512 devices in a mesh: group: 16 (over z_hi, y), tensor: 8 (over x, core), blk: 4 (over z_lo).
Axes of the slice: x: 4, y: 8, z: 8 (z_hi: 2, z_lo: 4; z = z_hi * 4 + z_lo), core: 2. Of those that a mesh axis runs over, the one named last changes fastest.
Arguments:
- trainer_input_rows: bfloat16 [2048, 5120], P('group', 'blk'), may hold values from -6 to 6
- policy_output_cotangent: bfloat16 [2048, 8192], P('group', 'tensor'), may hold values from -6 to 6
- down_factor: float32 [5120, 64], P('blk'), may hold values from -0.078125 to 0.078125
- up_factor: float32 [64, 8192], P(None, 'tensor'), may hold values from -0.3125 to 0.3125
- frozen_query_weight: bfloat16 [5120, 8192], P('blk', 'tensor'), may hold values from -0.078125 to 0.078125
- decode_hidden_state: bfloat16 [512, 5120], P('group', 'blk'), may hold values from -6 to 6
- cached_key_block: bfloat16 [512, 128, 1024], P(('group', 'blk'), None, 'tensor'), may hold values from -1000 to 1000, as said below
- cached_value_block: bfloat16 [512, 128, 1024], P(('group', 'blk'), None, 'tensor'), may hold values from -6 to 6
- incoming_key: bfloat16 [512, 1024], P(('group', 'blk'), 'tensor'), may hold values from -6 to 6
- incoming_value: bfloat16 [512, 1024], P(('group', 'blk'), 'tensor'), may hold values from -6 to 6
- cache_live_length: int32 [512], P(('group', 'blk')), may hold values from 1 to 128
Outputs:
- updated_down_factor: float32 [5120, 64], P('blk')
- updated_up_factor: float32 [64, 8192], P(None, 'tensor')
- attended: bfloat16 [512, 8192], P(('group', 'blk'), 'tensor')
The draws below stay inside these ranges and needn't reach their ends.
Inputs may be any that keep to these rules, and one draw needn't show every extreme that they name: `cached_key_block`: finite keys.
All inputs are finite; a program needn't handle non-finite values.
Results may differ from the reference program's by a relative error of at most 0.013.
Values sent between devices are 32-bit elements; how exact they have to be, the bound alone decides.
A program may use at most 64 MiB of HBM per device.

```python
import math
import jax
import jax.numpy as jnp
from jax import lax

MODEL_WIDTH = 5120
HEAD_SIZE = 128
ADAPTER_RANK = 64
R_DEV = 8
KVLEN = 128
QUERY_HEAD_COUNT = 64
KVH = 8
TOK_TRAIN = 2048
ROWS_TOTAL = 512
N_BLK = 4


def draw_cached_key_block(key, part):
    key = jax.random.fold_in(key, 7)
    first_key = jax.random.fold_in(key, 0)
    width = KVH * HEAD_SIZE
    base = jax.random.normal(first_key, (ROWS_TOTAL, KVLEN, width), jnp.float32)
    return base.astype(jnp.bfloat16)


def place_ends(result, stream_key, low, largest):
    spot = [jax.random.randint(jax.random.fold_in(stream_key, axis), (), 0, length) for axis, length in enumerate(result.shape)]
    widest = result.shape.index(max(result.shape))
    beside = spot[:widest] + [(spot[widest] + 1) % result.shape[widest]] + spot[widest + 1:]
    return result.at[tuple(spot)].set(low).at[tuple(beside)].set(largest)


def block_levels(rng, dims, cuts, least, high):
    def one(axis_at, shards_of):
        draws = jax.random.uniform(jax.random.fold_in(jax.random.fold_in(rng, 6), axis_at), (shards_of,), jnp.float32, least / len(cuts), high / len(cuts))
        return jnp.repeat(jnp.exp(draws), dims[axis_at] // shards_of).reshape((-1,) + (1,) * (len(dims) - axis_at - 1))

    loudness = one(*cuts[0])
    for cut in cuts[1:]:
        loudness = loudness * one(*cut)
    return loudness


def scatter_about(stream_key, dims, scale, most, cuts=(), held_as=jnp.bfloat16):
    result = jax.random.normal(stream_key, dims, jnp.float32) * scale
    if len(cuts) > 0:
        result = block_levels(stream_key, dims, cuts, -0.22, 0.18) * result
    return jnp.clip(result, min=-most, max=most).astype(held_as)


def setup_inputs(seed: int = 0) -> dict:
    key_of = jax.random.split(jax.random.key(seed), 12)
    return {
        "trainer_input_rows": scatter_about(key_of[0], (TOK_TRAIN, MODEL_WIDTH), 1.0, 6.0, ((0, 16), (1, 4))),
        "policy_output_cotangent": scatter_about(key_of[1], (TOK_TRAIN, QUERY_HEAD_COUNT * HEAD_SIZE), 1.0, 6.0, ((0, 16), (1, 8))),
        "down_factor": scatter_about(key_of[2], (MODEL_WIDTH, ADAPTER_RANK), MODEL_WIDTH ** -0.5, 0.078125, ((0, 4),), jnp.float32),
        "up_factor": scatter_about(key_of[3], (ADAPTER_RANK, QUERY_HEAD_COUNT * HEAD_SIZE), 0.02, 0.3125, ((1, 8),), jnp.float32),
        "frozen_query_weight": scatter_about(key_of[4], (MODEL_WIDTH, QUERY_HEAD_COUNT * HEAD_SIZE), MODEL_WIDTH ** -0.5, 0.078125, ((0, 4), (1, 8))),
        "decode_hidden_state": scatter_about(key_of[5], (ROWS_TOTAL, MODEL_WIDTH), 1.0, 6.0, ((0, 16), (1, 4))),
        "cached_key_block": draw_cached_key_block(jax.random.fold_in(key_of[11], 71), 0),
        "cached_value_block": scatter_about(key_of[7], (ROWS_TOTAL, KVLEN, KVH * HEAD_SIZE), 1.0, 6.0, ((0, 64), (2, 8))),
        "incoming_key": scatter_about(key_of[8], (ROWS_TOTAL, KVH * HEAD_SIZE), 1.0, 6.0, ((0, 64), (1, 8))),
        "incoming_value": scatter_about(key_of[9], (ROWS_TOTAL, KVH * HEAD_SIZE), 1.0, 6.0, ((0, 64), (1, 8))),
        "cache_live_length": place_ends(jax.random.randint(key_of[10], (ROWS_TOTAL,), 1, KVLEN + 1), jax.random.fold_in(key_of[10], 1), 1, KVLEN).astype(jnp.int32),
    }


adapter_scale = 2.0
learning_rate = 0.1
highest_precision = lax.Precision.HIGHEST

def attend(query, keys, values, own_key, own_value, lengths):
    count = query.shape[0]
    kv_heads = own_key.shape[1] // HEAD_SIZE
    span = keys.shape[1]
    adapter_factor = 1.0 / math.sqrt(HEAD_SIZE)
    query_wide = query.astype(jnp.float32).reshape(count, kv_heads, -1, HEAD_SIZE)
    key_wide = keys.astype(jnp.float32).reshape(count, span, kv_heads, HEAD_SIZE)
    value_wide = values.astype(jnp.float32).reshape(count, span, kv_heads, HEAD_SIZE)
    own_k = own_key.astype(jnp.float32).reshape(count, kv_heads, HEAD_SIZE)
    own_v = own_value.astype(jnp.float32).reshape(count, kv_heads, HEAD_SIZE)
    scores = jnp.einsum('nkgd,nlkd->nkgl', query_wide, key_wide) * adapter_factor
    live = (jnp.arange(span)[None, :] < lengths[:, None])[:, None, None, :]
    scores = jnp.where(live, scores, -1e+30)
    own_score = jnp.einsum('nkgd,nkd->nkg', query_wide, own_k) * adapter_factor
    peak = jnp.maximum(lax.optimization_barrier(jnp.max(scores, axis=-1)), own_score)
    expo = jnp.where(live, jnp.exp(scores - peak[..., None]), 0.0)
    own_expo = jnp.exp(own_score - peak)
    total = lax.optimization_barrier(jnp.sum(expo, axis=-1)) + own_expo
    weights = (expo / total[..., None]).astype(jnp.bfloat16)
    own_weight = (own_expo / total).astype(jnp.bfloat16)
    mixed = jnp.einsum('nkgl,nlkd->nkgd', weights.astype(jnp.float32), value_wide)
    mixed = mixed + own_weight.astype(jnp.float32)[..., None] * own_v[:, :, None, :]
    return mixed.reshape(count, -1).astype(jnp.bfloat16)

def reference(trainer_input_rows, policy_output_cotangent, down_factor, up_factor, frozen_query_weight, decode_hidden_state, cached_key_block, cached_value_block, incoming_key, incoming_value, cache_live_length):
    input_rows_flat = trainer_input_rows.astype(jnp.float32)
    cotangent_rows = policy_output_cotangent.astype(jnp.float32)
    tokens = input_rows_flat.shape[0]
    rank_product = jnp.dot(input_rows_flat, down_factor, precision=highest_precision)
    backward_projection = jnp.dot(cotangent_rows, up_factor.T, precision=highest_precision)
    down_gradient = jnp.dot(input_rows_flat.T, backward_projection, precision=highest_precision) * (adapter_scale / tokens)
    up_gradient = jnp.dot(rank_product.T, cotangent_rows, precision=highest_precision) * (adapter_scale / tokens)
    updated_down_factor = down_factor - learning_rate * down_gradient
    updated_up_factor = up_factor - learning_rate * up_gradient
    hidden_wide = decode_hidden_state.astype(jnp.float32)
    adapted = jnp.dot(jnp.dot(hidden_wide, updated_down_factor, precision=highest_precision), updated_up_factor, precision=highest_precision)
    query = jnp.dot(decode_hidden_state, frozen_query_weight, preferred_element_type=jnp.float32) + adapter_scale * adapted
    query = query.astype(jnp.bfloat16)
    block = R_DEV * N_BLK
    blocks = query.shape[0] // block

    def one_block(items):
        return attend(*items)
    pieces = (query.reshape(blocks, block, -1), cached_key_block.reshape(blocks, block, cached_key_block.shape[1], -1), cached_value_block.reshape(blocks, block, cached_value_block.shape[1], -1), incoming_key.reshape(blocks, block, -1), incoming_value.reshape(blocks, block, -1), cache_live_length.reshape(blocks, block))
    attended = lax.map(one_block, pieces).reshape(query.shape[0], -1)
    return (updated_down_factor, updated_up_factor, attended)
```

```python
import math

import jax
import jax.numpy as jnp
from jax import lax
from jax.experimental import pallas as pl
from jax.experimental.pallas import tpu as pltpu
from jax.sharding import PartitionSpec as P

MESH = pl.DeviceIdType.MESH
f32, bf16 = jnp.float32, jnp.bfloat16

adapter_scale = 2.0
learning_rate = 0.1
TOKENS = 2048
STEP = learning_rate * adapter_scale / TOKENS
OWNERS = 5
FAR_FIRST = (4, 5, 3, 7, 6, 2, 1)


def split(v):
    hi = v.astype(bf16)
    return hi, (v - hi.astype(f32)).astype(bf16)


def dot_nt(p, q):
    return lax.dot_general(p, q, (((1,), (1,)), ((), ())), preferred_element_type=f32)


def dot_nn(p, q):
    return jnp.dot(p, q, preferred_element_type=f32)


def twice(dot, v, q):
    rows = v.shape[0]
    hi, lo = split(v)
    both = dot(jnp.concatenate([hi, lo], axis=0), q)
    return both[:rows] + both[rows:]


def exchange(
    x_any, c_any, at_any, b_any, w_any, h_any, k_any, v_any, ik_any, iv_any, len_any,
    at_out, b_out, att_out,
    x, c, at, bu, w, hid, kc, vc, ik, iv, lens,
    p_part, p_recv, a_part, a1_recv, a_half, a2_send, a2_recv, a_full,
    b_part, b1_recv, b_line, b_full,
    hw_part, hw_recv, hx_send, hx_recv, u_send, u_all, fold,
    in_sem, p_s, p_r, a1_s, a1_r, a2_s, a2_r, a3_s, a3_r, a4_s, a4_r, a5_s, a5_r,
    b1_s, b1_r, b2_s, b2_r, b3_s, b3_r, hw_s, hw_r, hx_s, hx_r, u_s, u_r,
):
    g, t, b = lax.axis_index("group"), lax.axis_index("tensor"), lax.axis_index("blk")
    zh, y = lax.div(g, 8), lax.rem(g, 8)
    core = lax.rem(t, 2)
    z = zh * 4 + b
    y_first = core == 0
    m, n = jnp.where(y_first, y, z), jnp.where(y_first, z, y)

    def at_yt(dy, dt):
        return (zh * 8 + (y ^ dy), t ^ dt, b)

    def at_zt(dz, dt):
        far = z ^ dz
        return (lax.div(far, 4) * 8 + y, t ^ dt, lax.rem(far, 4))

    def at_y(d):
        return at_yt(d, 0)

    def at_z(d):
        return at_zt(d, 0)

    def at_t(d):
        return (g, t ^ d, b)

    def first(d):
        return tuple(jnp.where(y_first, p, q) for p, q in zip(at_y(d), at_z(d)))

    def second(d):
        return tuple(jnp.where(y_first, q, p) for p, q in zip(at_y(d), at_z(d)))

    barrier = pltpu.get_barrier_semaphore()
    for d in FAR_FIRST:
        for device in (at_t(d), at_y(d), at_z(d)):
            pl.semaphore_signal(barrier, inc=1, device_id=device, device_id_type=MESH)

    loads = [
        pltpu.make_async_copy(src, dst, in_sem.at[i])
        for i, (src, dst) in enumerate(
            zip(
                (c_any, b_any, x_any, at_any, h_any, w_any, k_any, v_any, ik_any, iv_any, len_any),
                (c, bu, x, at, hid, w, kc, vc, ik, iv, lens),
            )
        )
    ]
    for copy in loads:
        copy.start()

    arrivals, departures = {}, []

    def send(name, src, dst, sems, i, device):
        copy = pltpu.make_async_remote_copy(
            src_ref=src, dst_ref=dst, send_sem=sems[0].at[i], recv_sem=sems[1].at[i],
            device_id=device, device_id_type=MESH,
        )
        copy.start()
        arrivals.setdefault(name, []).append(copy.wait_recv)
        departures.append(copy.wait_send)

    def send_if(name, out, src, come, dst, sems, i, device):
        copy = pltpu.make_async_remote_copy(
            src_ref=src, dst_ref=dst, send_sem=sems[0].at[i], recv_sem=sems[1].at[i],
            device_id=device, device_id_type=MESH,
        )
        pl.when(out)(copy.start)
        arrivals.setdefault(name, []).append(lambda: pl.when(come)(copy.wait_recv))
        departures.append(lambda: pl.when(out)(copy.wait_send))

    def arrive(name):
        for wait in arrivals.pop(name):
            wait()

    def rows(d):
        return pl.ds(pl.multiple_of(d * 8, 8), 8)

    def hidden_chunk(i):
        cols = pl.ds(i * 256, 256)
        hw_part[:, :, cols] = dot_nn(hid[...], w[:, cols]).reshape(4, 8, 256)

    loads[0].wait()
    loads[1].wait()
    p_part[...] = twice(dot_nt, bu[...], c[...]).reshape(8, 8, 128)

    loads[2].wait()
    loads[3].wait()
    low = twice(dot_nt, at[...], x[...])
    grad_b = twice(dot_nn, low, c[...])
    for i in range(8):
        for j in range(8):
            place = jnp.where(y_first, j * 8 + i, i * 8 + j)
            b_part[pl.ds(place, 1)] = grad_b[i * 8 : i * 8 + 8, j * 128 : j * 128 + 128].reshape(1, 8, 128)
    loads[4].wait()
    hx_send[...] = hid[...].astype(f32).reshape(8, 4, 1280)

    pl.semaphore_wait(barrier, 21)
    for d in FAR_FIRST:
        send("p", p_part.at[t ^ d], p_recv.at[d - 1], (p_s, p_r), d - 1, at_t(d))
    for d in FAR_FIRST:
        send("b1", b_part.at[rows(m ^ d)], b1_recv.at[d - 1], (b1_s, b1_r), d - 1, first(d))

    send("hx", hx_send.at[t], hx_recv.at[t], (hx_s, hx_r), 0, at_z(4))

    into = lax.broadcasted_iota(jnp.int32, (1024, 64), 0)
    out = lax.broadcasted_iota(jnp.int32, (1024, 64), 1)
    hit = (lax.div(into, 128) == lax.div(out, 8)) & (lax.rem(into, 8) == lax.rem(out, 8))
    fold[...] = jnp.where(hit, 1.0, 0.0).astype(bf16)

    loads[5].wait()
    hidden_chunk(0)
    hidden_chunk(1)

    arrive("p")
    back = p_part[t]
    for d in range(7):
        back = back + p_recv[d]
    grad_a = twice(dot_nn, back, x[...])
    for i in range(OWNERS):
        a_part[i] = grad_a[:, i * 256 : i * 256 + 256]
    owner = y < OWNERS
    piece = jnp.minimum(y, OWNERS - 1)
    for d in FAR_FIRST:
        send_if("a1", (y ^ d) < OWNERS, a_part.at[jnp.minimum(y ^ d, OWNERS - 1)], owner, a1_recv.at[d - 1], (a1_s, a1_r), d - 1, at_y(d))
    hidden_chunk(2)
    hidden_chunk(3)

    old = at[rows(t), pl.ds(pl.multiple_of(piece * 256, 256), 256)]

    @pl.when(owner)
    def _():
        for wait in arrivals["a1"]:
            wait()
        total = a_part[piece]
        for d in range(7):
            total = total + a1_recv[d]
        a2_send[...] = total
        a_half[piece] = jnp.where(zh == 0, old, 0.0) - STEP * total

    arrivals.pop("a1")
    for d in FAR_FIRST:
        send_if("a3", owner, a_half.at[piece], (y ^ d) < OWNERS, a_half.at[piece], (a3_s, a3_r), d - 1, at_y(d))
    send_if("a2", owner, a2_send, owner, a2_recv, (a2_s, a2_r), 0, at_z(4))
    arrive("hx")
    for d in FAR_FIRST:
        send("hx2", hx_recv.at[t], hx_recv.at[t], (hx_s, hx_r), d, at_t(d))

    arrive("b1")
    total = b_part[rows(m)]
    for d in range(7):
        total = total + b1_recv[d]
    b_line[n] = total
    for d in FAR_FIRST:
        send("b2", b_line.at[n], b_line.at[n], (b2_s, b2_r), d - 1, second(d))
    for d in (3, 2, 1):
        send("hw", hw_part.at[b ^ d], hw_recv.at[d - 1], (hw_s, hw_r), d - 1, at_z(d))

    @pl.when(owner)
    def _():
        for wait in arrivals["a2"]:
            wait()
        a_full[t, piece] = old - STEP * (a2_send[...] + a2_recv[...])

    arrivals.pop("a2")
    for i, dt in enumerate((4, 2, 6, 0)):
        for d in FAR_FIRST + (0,):
            if d or dt:
                send_if(
                    "a4" + str(dt), owner, a_full.at[t, piece], (y ^ d) < OWNERS, a_full.at[t, piece], (a4_s, a4_r), i * 8 + d, at_yt(d, dt)
                )

    arrive("a3")
    arrive("hx2")
    near = jnp.zeros((64, 128), f32)
    both = jnp.concatenate([hid[...], hx_recv[...].reshape(32, 1280).astype(bf16)], axis=0)
    for i in range(OWNERS):
        hi, lo = split(jnp.concatenate([a_half[i]] * 8, axis=0))
        near = near + dot_nt(both[:, i * 256 : i * 256 + 256], jnp.concatenate([hi, lo], axis=0))
    lane = lax.broadcasted_iota(jnp.int32, (64, 128), 1)
    row = lax.broadcasted_iota(jnp.int32, (64, 128), 0)
    near = jnp.where(lax.rem(lax.div(lane, 8), 8) == lax.rem(row, 8), near, 0.0).reshape(2, 4, 8, 128)
    near = jnp.sum(near, axis=2, keepdims=True)
    u_send[pl.ds(zh * 4, 4)] = near[0]
    u_send[pl.ds(4 - zh * 4, 4)] = near[1]
    u_all[t * 8 + z] = u_send[z]
    for dz in (4, 5, 3, 7, 6, 2, 1, 0):
        for dt in (4, 5, 2, 3, 6, 7, 1, 0):
            if dz or dt:
                copy = pltpu.make_async_remote_copy(
                    src_ref=u_send.at[z ^ dz], dst_ref=u_all.at[t * 8 + z], send_sem=u_s, recv_sem=u_r,
                    device_id=at_zt(dz, dt), device_id_type=MESH,
                )
                copy.start()

    arrive("b2")
    total = b_line[0]
    for i in range(1, 8):
        total = total + b_line[i]
    for i in range(8):
        line, col = jnp.where(y_first, i, m), jnp.where(y_first, m, i)
        tile = bu[rows(line), pl.ds(pl.multiple_of(col * 128, 128), 128)]
        b_full[m, i] = tile - STEP * total[i]
    for d in FAR_FIRST:
        send("b3", b_full.at[m], b_full.at[m], (b3_s, b3_r), d - 1, first(d))

    arrive("hw")
    base = hw_part[b]
    for d in range(3):
        base = base + hw_recv[d]

    for i, dt in enumerate((0, 6, 2, 4)):
        arrive("a4" + str(dt))
        send("a5", a_full.at[t ^ dt], a_full.at[t ^ dt], (a5_s, a5_r), i, at_t(1))

    most = u_all.at[pl.ds(0, 63)]
    pltpu.make_async_copy(most, most, u_r).wait()
    slices = jnp.sum(u_all[...].reshape(8, 8, 1, 128), axis=1)
    lane = lax.broadcasted_iota(jnp.int32, (8, 128), 1)
    row = lax.broadcasted_iota(jnp.int32, (8, 128), 0)
    wide = jnp.concatenate(
        [jnp.where(lax.rem(lax.div(lane, 8), 8) == row, jnp.broadcast_to(slices[i], (8, 128)), 0.0) for i in range(8)], axis=1
    )
    hidden_low = twice(dot_nn, wide, fold[...])

    arrive("b3")
    for i in range(8):
        for j in range(8):
            first_at, second_at = jnp.where(y_first, j, i), jnp.where(y_first, i, j)
            b_out[i * 8 : i * 8 + 8, j * 128 : j * 128 + 128] = b_full[first_at, second_at]

    b_hi, b_lo = split(b_out[...])
    hi, lo = split(hidden_low)
    both = dot_nn(jnp.concatenate([hi, lo], axis=0), b_hi)
    query = base + adapter_scale * (both[:8] + both[8:] + dot_nn(hi, b_lo))

    for copy in loads[6:]:
        copy.wait()
    heads = jnp.concatenate([query[:, i * 128 : i * 128 + 128] for i in range(8)], axis=0).astype(bf16)
    scale = 1.0 / math.sqrt(128)
    scores = (dot_nt(heads, kc[...]) * scale).reshape(8, 8, 1024)
    row = lax.broadcasted_iota(jnp.int32, (8, 128), 0)
    slot = lax.broadcasted_iota(jnp.int32, (8, 128), 1)
    live = jnp.concatenate(
        [jnp.where((row == i) & (slot < lens[i]), 1.0, 0.0) for i in range(8)], axis=1
    )[None]
    live = jnp.broadcast_to(live, scores.shape) > 0.5
    scores = jnp.where(live, scores, -1e30)
    own_k = ik[...].astype(f32)[None]
    own = jnp.sum(heads.astype(f32).reshape(8, 8, 128) * own_k, axis=-1, keepdims=True) * scale
    peak = jnp.maximum(jnp.max(scores, axis=-1, keepdims=True), own)
    expo = jnp.where(live, jnp.exp(scores - peak), 0.0)
    own_expo = jnp.exp(own - peak)
    total = jnp.sum(expo, axis=-1, keepdims=True) + own_expo
    weights = (expo / total).astype(bf16).reshape(64, 1024)
    own_weight = (own_expo / total).astype(bf16).astype(f32)
    mixed = dot_nn(weights, vc[...]).reshape(8, 8, 128) + own_weight * iv[...].astype(f32)[None]
    mixed = mixed.astype(bf16)
    for i in range(8):
        att_out[:, i * 128 : i * 128 + 128] = mixed[i]

    arrive("a5")
    for i in range(8):
        for j in range(OWNERS):
            at_out[i * 8 : i * 8 + 8, j * 256 : j * 256 + 256] = a_full[i, j]

    for wait in departures:
        wait()
    pltpu.make_async_copy(most, most, u_s).wait()


def finish(at_in, b_in, att_in, at_out, b_out, att_out, sem):
    stores = [
        pltpu.make_async_copy(src, dst, sem.at[i])
        for i, (src, dst) in enumerate(((at_in, at_out), (b_in, b_out), (att_in, att_out)))
    ]
    for copy in stores:
        copy.start()
    for copy in stores:
        copy.wait()


def local(x, c, a, bu, w, hid, keys, values, ik, iv, lens):
    vm, dma = pltpu.VMEM, pltpu.SemaphoreType.DMA
    slots = keys.shape[0] * keys.shape[1]
    hbm = pl.BlockSpec(memory_space=pltpu.HBM)
    vmem = pl.BlockSpec(memory_space=pltpu.VMEM)

    def two(i):
        return [dma((i,)), dma((i,))]

    outs = (
        jax.ShapeDtypeStruct((64, 1280), f32),
        jax.ShapeDtypeStruct((64, 1024), f32),
        jax.ShapeDtypeStruct((8, 1024), bf16),
    )
    arrays = (x, c, a.T, bu, w, hid, keys.reshape(slots, 128), values.reshape(slots, 128), ik, iv, lens)
    new = pl.pallas_call(
        exchange,
        out_shape=outs,
        in_specs=[hbm] * 11,
        out_specs=(vmem,) * 3,
        scratch_shapes=[
            vm((128, 1280), bf16), vm((128, 1024), bf16), vm((64, 1280), f32), vm((64, 1024), f32),
            vm((1280, 1024), bf16), vm((32, 1280), bf16), vm((slots, 128), bf16), vm((slots, 128), bf16),
            vm((8, 128), bf16), vm((8, 128), bf16), pltpu.SMEM((8,), jnp.int32),
            vm((8, 8, 128), f32), vm((7, 8, 128), f32),
            vm((OWNERS, 8, 256), f32), vm((7, 8, 256), f32),
            vm((OWNERS, 8, 256), f32), vm((8, 256), f32), vm((8, 256), f32), vm((8, OWNERS, 8, 256), f32),
            vm((64, 8, 128), f32), vm((7, 8, 8, 128), f32), vm((8, 8, 8, 128), f32), vm((8, 8, 8, 128), f32),
            vm((4, 8, 1024), f32), vm((3, 8, 1024), f32),
            vm((8, 4, 1280), f32), vm((8, 4, 1280), f32),
            vm((8, 1, 128), f32), vm((64, 1, 128), f32), vm((1024, 64), bf16),
            dma((11,)), *two(7), *two(7), *two(1), *two(7), *two(32), *two(4),
            *two(7), *two(7), *two(7), *two(3), *two(8), dma, dma,
        ],
        compiler_params=pltpu.CompilerParams(
            collective_id=0, has_side_effects=True, vmem_limit_bytes=24 * 2**20
        ),
        name="exchange",
    )(*(pltpu.with_memory_space_constraint(v, pltpu.HBM) for v in arrays))
    at_new, b_new, attended = pl.pallas_call(
        finish,
        out_shape=outs,
        in_specs=[vmem] * 3,
        out_specs=(hbm,) * 3,
        scratch_shapes=[dma((3,))],
        compiler_params=pltpu.CompilerParams(vmem_limit_bytes=24 * 2**20),
        name="finish",
    )(*new)
    return at_new.T, b_new, attended


def solution(mesh):
    return jax.shard_map(
        local,
        mesh=mesh,
        in_specs=(
            P("group", "blk"),
            P("group", "tensor"),
            P("blk", None),
            P(None, "tensor"),
            P("blk", "tensor"),
            P("group", "blk"),
            P(("group", "blk"), None, "tensor"),
            P(("group", "blk"), None, "tensor"),
            P(("group", "blk"), "tensor"),
            P(("group", "blk"), "tensor"),
            P(("group", "blk")),
        ),
        out_specs=(P("blk", None), P(None, "tensor"), P(("group", "blk"), "tensor")),
        check_vma=False,
    )
```

```python
import math

import jax
import jax.numpy as jnp
from jax import lax
from jax.experimental import pallas as pl
from jax.experimental.pallas import tpu as pltpu
from jax.sharding import PartitionSpec as P

MESH = pl.DeviceIdType.MESH
f32, bf16 = jnp.float32, jnp.bfloat16

adapter_scale = 2.0
learning_rate = 0.1
TOKENS = 2048
STEP = learning_rate * adapter_scale / TOKENS
OWNERS = 5
FAR_FIRST = (4, 5, 3, 7, 6, 2, 1)
STAGES = ("p", "b1", "hx", "hx2", "a1", "a2", "a3", "b2", "hw", "a40", "a42", "a44", "a46", "u", "b3", "a5")


def split(v):
    hi = v.astype(bf16)
    return hi, (v - hi.astype(f32)).astype(bf16)


def dot_nt(p, q):
    return lax.dot_general(p, q, (((1,), (1,)), ((), ())), preferred_element_type=f32)


def dot_nn(p, q):
    return jnp.dot(p, q, preferred_element_type=f32)


def twice(dot, v, q):
    rows = v.shape[0]
    hi, lo = split(v)
    both = dot(jnp.concatenate([hi, lo], axis=0), q)
    return both[:rows] + both[rows:]


def exchange(
    x_any, c_any, at_any, b_any, w_any, h_any, k_any, v_any, ik_any, iv_any, len_any,
    at_out, b_out, att_out,
    x, c, at, bu, w, hid, kc, vc, ik, iv, lens,
    p_part, p_recv, a_part, a1_recv, a_half, a2_send, a2_recv, a_full,
    b_part, b1_recv, b_line, b_full,
    hw_part, hw_recv, hx_send, hx_recv, u_send, u_all, fold,
    in_sem, sems,
):
    g, t, b = lax.axis_index("group"), lax.axis_index("tensor"), lax.axis_index("blk")
    zh, y = lax.div(g, 8), lax.rem(g, 8)
    core = lax.rem(t, 2)
    z = zh * 4 + b
    y_first = core == 0
    m, n = jnp.where(y_first, y, z), jnp.where(y_first, z, y)

    def at_yt(dy, dt):
        return (zh * 8 + (y ^ dy), t ^ dt, b)

    def at_zt(dz, dt):
        far = z ^ dz
        return (lax.div(far, 4) * 8 + y, t ^ dt, lax.rem(far, 4))

    def at_y(d):
        return at_yt(d, 0)

    def at_z(d):
        return at_zt(d, 0)

    def at_t(d):
        return (g, t ^ d, b)

    def first(d):
        return tuple(jnp.where(y_first, p, q) for p, q in zip(at_y(d), at_z(d)))

    def second(d):
        return tuple(jnp.where(y_first, q, p) for p, q in zip(at_y(d), at_z(d)))

    barrier = pltpu.get_barrier_semaphore()
    for d in FAR_FIRST:
        for device in (at_t(d), at_y(d), at_z(d)):
            pl.semaphore_signal(barrier, inc=1, device_id=device, device_id_type=MESH)

    loads = [
        pltpu.make_async_copy(src, dst, in_sem.at[i])
        for i, (src, dst) in enumerate(
            zip(
                (c_any, b_any, x_any, at_any, h_any, w_any, k_any, v_any, ik_any, iv_any, len_any),
                (c, bu, x, at, hid, w, kc, vc, ik, iv, lens),
            )
        )
    ]
    for copy in loads:
        copy.start()

    def leaves(stage):
        return sems.at[2 * STAGES.index(stage)]

    def comes(stage):
        return sems.at[2 * STAGES.index(stage) + 1]

    def send(stage, src, dst, device):
        pltpu.make_async_remote_copy(
            src_ref=src, dst_ref=dst, send_sem=leaves(stage), recv_sem=comes(stage),
            device_id=device, device_id_type=MESH,
        ).start()

    def wait(sem, ref):
        pltpu.make_async_copy(ref, ref, sem).wait()

    def wait_if(case, sem, ref, otherwise):
        pl.when(case)(lambda: wait(sem, ref))
        if otherwise is not None:
            pl.when(jnp.logical_not(case))(lambda: wait(sem, otherwise))

    def rows(d):
        return pl.ds(pl.multiple_of(d * 8, 8), 8)

    def hidden_chunk(i):
        cols = pl.ds(i * 256, 256)
        hw_part[:, :, cols] = dot_nn(hid[...], w[:, cols]).reshape(4, 8, 256)

    loads[0].wait()
    loads[1].wait()
    p_part[...] = twice(dot_nt, bu[...], c[...]).reshape(8, 8, 128)

    loads[2].wait()
    loads[3].wait()
    low = twice(dot_nt, at[...], x[...])
    grad_b = twice(dot_nn, low, c[...])
    for i in range(8):
        for j in range(8):
            place = jnp.where(y_first, j * 8 + i, i * 8 + j)
            b_part[pl.ds(place, 1)] = grad_b[i * 8 : i * 8 + 8, j * 128 : j * 128 + 128].reshape(1, 8, 128)
    loads[4].wait()
    hx_send[...] = hid[...].astype(f32).reshape(8, 4, 1280)

    pl.semaphore_wait(barrier, 21)
    for d in FAR_FIRST:
        send("p", p_part.at[t ^ d], p_recv.at[d - 1], at_t(d))
    for d in FAR_FIRST:
        send("b1", b_part.at[rows(m ^ d)], b1_recv.at[d - 1], first(d))

    send("hx", hx_send.at[t], hx_recv.at[t], at_z(4))

    into = lax.broadcasted_iota(jnp.int32, (1024, 64), 0)
    out = lax.broadcasted_iota(jnp.int32, (1024, 64), 1)
    hit = (lax.div(into, 128) == lax.div(out, 8)) & (lax.rem(into, 8) == lax.rem(out, 8))
    fold[...] = jnp.where(hit, 1.0, 0.0).astype(bf16)

    loads[5].wait()
    hidden_chunk(0)
    hidden_chunk(1)

    wait(comes("p"), p_recv)
    back = p_part[t]
    for d in range(7):
        back = back + p_recv[d]
    grad_a = twice(dot_nn, back, x[...])
    for i in range(OWNERS):
        a_part[i] = grad_a[:, i * 256 : i * 256 + 256]
    owner = y < OWNERS
    piece = jnp.minimum(y, OWNERS - 1)
    for d in FAR_FIRST:
        far = jnp.minimum(y ^ d, OWNERS - 1)
        pl.when((y ^ d) < OWNERS)(lambda d=d, far=far: send("a1", a_part.at[far], a1_recv.at[d - 1], at_y(d)))
    hidden_chunk(2)
    hidden_chunk(3)

    old = at[rows(t), pl.ds(pl.multiple_of(piece * 256, 256), 256)]

    @pl.when(owner)
    def _():
        wait(comes("a1"), a1_recv)
        total = a_part[piece]
        for d in range(7):
            total = total + a1_recv[d]
        a2_send[...] = total
        a_half[piece] = jnp.where(zh == 0, old, 0.0) - STEP * total
        for d in FAR_FIRST:
            send("a3", a_half.at[piece], a_half.at[piece], at_y(d))
        send("a2", a2_send, a2_recv, at_z(4))


    wait(comes("hx"), hx_recv.at[t])
    for d in FAR_FIRST:
        send("hx2", hx_recv.at[t], hx_recv.at[t], at_t(d))

    wait(comes("b1"), b1_recv)
    total = b_part[rows(m)]
    for d in range(7):
        total = total + b1_recv[d]
    b_line[n] = total
    for d in FAR_FIRST:
        send("b2", b_line.at[n], b_line.at[n], second(d))
    for d in (3, 2, 1):
        send("hw", hw_part.at[b ^ d], hw_recv.at[d - 1], at_z(d))

    @pl.when(owner)
    def _():
        wait(comes("a2"), a2_recv)
        a_full[t, piece] = old - STEP * (a2_send[...] + a2_recv[...])
        for dt in (4, 2, 6, 0):
            for d in FAR_FIRST + (0,):
                if d or dt:
                    send("a4" + str(dt), a_full.at[t, piece], a_full.at[t, piece], at_yt(d, dt))


    wait_if(owner, comes("a3"), a_half.at[pl.ds(0, OWNERS - 1)], a_half)
    wait(comes("hx2"), hx_recv.at[pl.ds(0, 7)])
    near = jnp.zeros((64, 128), f32)
    both = jnp.concatenate([hid[...], hx_recv[...].reshape(32, 1280).astype(bf16)], axis=0)
    for i in range(OWNERS):
        hi, lo = split(jnp.concatenate([a_half[i]] * 8, axis=0))
        near = near + dot_nt(both[:, i * 256 : i * 256 + 256], jnp.concatenate([hi, lo], axis=0))
    lane = lax.broadcasted_iota(jnp.int32, (64, 128), 1)
    row = lax.broadcasted_iota(jnp.int32, (64, 128), 0)
    near = jnp.where(lax.rem(lax.div(lane, 8), 8) == lax.rem(row, 8), near, 0.0).reshape(2, 4, 8, 128)
    near = jnp.sum(near, axis=2, keepdims=True)
    u_send[pl.ds(zh * 4, 4)] = near[0]
    u_send[pl.ds(4 - zh * 4, 4)] = near[1]
    u_all[t * 8 + z] = u_send[z]
    for dz in (4, 5, 3, 7, 6, 2, 1, 0):
        for dt in (4, 5, 2, 3, 6, 7, 1, 0):
            if dz or dt:
                copy = pltpu.make_async_remote_copy(
                    src_ref=u_send.at[z ^ dz], dst_ref=u_all.at[t * 8 + z], send_sem=leaves("u"), recv_sem=comes("u"),
                    device_id=at_zt(dz, dt), device_id_type=MESH,
                )
                copy.start()

    wait(comes("b2"), b_line.at[pl.ds(0, 7)])
    total = b_line[0]
    for i in range(1, 8):
        total = total + b_line[i]
    for i in range(8):
        line, col = jnp.where(y_first, i, m), jnp.where(y_first, m, i)
        tile = bu[rows(line), pl.ds(pl.multiple_of(col * 128, 128), 128)]
        b_full[m, i] = tile - STEP * total[i]
    for d in FAR_FIRST:
        send("b3", b_full.at[m], b_full.at[m], first(d))

    for i, dt in enumerate((0, 6, 2, 4)):
        if dt:
            wait(comes("a4" + str(dt)), a_full.at[t ^ dt])
        else:
            wait_if(owner, comes("a40"), a_full.at[t, pl.ds(0, OWNERS - 1)], a_full.at[t])
        send("a5", a_full.at[t ^ dt], a_full.at[t ^ dt], at_t(1))

    wait(comes("hw"), hw_recv)
    base = hw_part[b]
    for d in range(3):
        base = base + hw_recv[d]

    most = u_all.at[pl.ds(0, 63)]
    wait(comes("u"), most)
    slices = jnp.sum(u_all[...].reshape(8, 8, 1, 128), axis=1)
    lane = lax.broadcasted_iota(jnp.int32, (8, 128), 1)
    row = lax.broadcasted_iota(jnp.int32, (8, 128), 0)
    wide = jnp.concatenate(
        [jnp.where(lax.rem(lax.div(lane, 8), 8) == row, jnp.broadcast_to(slices[i], (8, 128)), 0.0) for i in range(8)], axis=1
    )
    hidden_low = twice(dot_nn, wide, fold[...])

    wait(comes("b3"), b_full.at[pl.ds(0, 7)])
    for i in range(8):
        for j in range(8):
            first_at, second_at = jnp.where(y_first, j, i), jnp.where(y_first, i, j)
            b_out[i * 8 : i * 8 + 8, j * 128 : j * 128 + 128] = b_full[first_at, second_at]

    b_hi, b_lo = split(b_out[...])
    hi, lo = split(hidden_low)
    both = dot_nn(jnp.concatenate([hi, lo], axis=0), b_hi)
    query = base + adapter_scale * (both[:8] + both[8:] + dot_nn(hi, b_lo))

    for copy in loads[6:]:
        copy.wait()
    heads = jnp.concatenate([query[:, i * 128 : i * 128 + 128] for i in range(8)], axis=0).astype(bf16)
    scale = 1.0 / math.sqrt(128)
    scores = (dot_nt(heads, kc[...]) * scale).reshape(8, 8, 1024)
    row = lax.broadcasted_iota(jnp.int32, (8, 128), 0)
    slot = lax.broadcasted_iota(jnp.int32, (8, 128), 1)
    live = jnp.concatenate(
        [jnp.where((row == i) & (slot < lens[i]), 1.0, 0.0) for i in range(8)], axis=1
    )[None]
    live = jnp.broadcast_to(live, scores.shape) > 0.5
    scores = jnp.where(live, scores, -1e30)
    own_k = ik[...].astype(f32)[None]
    own = jnp.sum(heads.astype(f32).reshape(8, 8, 128) * own_k, axis=-1, keepdims=True) * scale
    peak = jnp.maximum(jnp.max(scores, axis=-1, keepdims=True), own)
    expo = jnp.where(live, jnp.exp(scores - peak), 0.0)
    own_expo = jnp.exp(own - peak)
    total = jnp.sum(expo, axis=-1, keepdims=True) + own_expo
    weights = (expo / total).astype(bf16).reshape(64, 1024)
    own_weight = (own_expo / total).astype(bf16).astype(f32)
    mixed = dot_nn(weights, vc[...]).reshape(8, 8, 128) + own_weight * iv[...].astype(f32)[None]
    mixed = mixed.astype(bf16)
    for i in range(8):
        att_out[:, i * 128 : i * 128 + 128] = mixed[i]

    wait(comes("a5"), a_full.at[pl.ds(0, 4)])
    for i in range(8):
        for j in range(OWNERS):
            at_out[i * 8 : i * 8 + 8, j * 256 : j * 256 + 256] = a_full[i, j]

    for stage, ref in (
        ("p", p_recv), ("b1", b1_recv), ("hx", hx_recv.at[t]), ("hx2", hx_recv.at[pl.ds(0, 7)]),
        ("b2", b_line.at[pl.ds(0, 7)]), ("hw", hw_recv), ("u", most), ("b3", b_full.at[pl.ds(0, 7)]),
        ("a5", a_full.at[pl.ds(0, 4)]),
    ):
        wait(leaves(stage), ref)
    wait_if(owner, leaves("a1"), a_part.at[pl.ds(0, OWNERS - 1)], a_part)

    @pl.when(owner)
    def _():
        wait(leaves("a3"), a1_recv)
        wait(leaves("a2"), a2_recv)
        wait(leaves("a40"), a1_recv)
        for dt in (2, 4, 6):
            wait(leaves("a4" + str(dt)), b_line.at[pl.ds(0, 2)])


def finish(at_in, b_in, att_in, at_out, b_out, att_out, sem):
    stores = [
        pltpu.make_async_copy(src, dst, sem.at[i])
        for i, (src, dst) in enumerate(((at_in, at_out), (b_in, b_out), (att_in, att_out)))
    ]
    for copy in stores:
        copy.start()
    for copy in stores:
        copy.wait()


def local(x, c, a, bu, w, hid, keys, values, ik, iv, lens):
    vm, dma = pltpu.VMEM, pltpu.SemaphoreType.DMA
    slots = keys.shape[0] * keys.shape[1]
    hbm = pl.BlockSpec(memory_space=pltpu.HBM)
    vmem = pl.BlockSpec(memory_space=pltpu.VMEM)

    outs = (
        jax.ShapeDtypeStruct((64, 1280), f32),
        jax.ShapeDtypeStruct((64, 1024), f32),
        jax.ShapeDtypeStruct((8, 1024), bf16),
    )
    arrays = (x, c, a.T, bu, w, hid, keys.reshape(slots, 128), values.reshape(slots, 128), ik, iv, lens)
    new = pl.pallas_call(
        exchange,
        out_shape=outs,
        in_specs=[hbm] * 11,
        out_specs=(vmem,) * 3,
        scratch_shapes=[
            vm((128, 1280), bf16), vm((128, 1024), bf16), vm((64, 1280), f32), vm((64, 1024), f32),
            vm((1280, 1024), bf16), vm((32, 1280), bf16), vm((slots, 128), bf16), vm((slots, 128), bf16),
            vm((8, 128), bf16), vm((8, 128), bf16), pltpu.SMEM((8,), jnp.int32),
            vm((8, 8, 128), f32), vm((7, 8, 128), f32),
            vm((OWNERS, 8, 256), f32), vm((7, 8, 256), f32),
            vm((OWNERS, 8, 256), f32), vm((8, 256), f32), vm((8, 256), f32), vm((8, OWNERS, 8, 256), f32),
            vm((64, 8, 128), f32), vm((7, 8, 8, 128), f32), vm((8, 8, 8, 128), f32), vm((8, 8, 8, 128), f32),
            vm((4, 8, 1024), f32), vm((3, 8, 1024), f32),
            vm((8, 4, 1280), f32), vm((8, 4, 1280), f32),
            vm((8, 1, 128), f32), vm((64, 1, 128), f32), vm((1024, 64), bf16),
            dma((11,)), dma((2 * len(STAGES),)),
        ],
        compiler_params=pltpu.CompilerParams(
            collective_id=0, has_side_effects=True, vmem_limit_bytes=24 * 2**20
        ),
        name="exchange",
    )(*(pltpu.with_memory_space_constraint(v, pltpu.HBM) for v in arrays))
    at_new, b_new, attended = pl.pallas_call(
        finish,
        out_shape=outs,
        in_specs=[vmem] * 3,
        out_specs=(hbm,) * 3,
        scratch_shapes=[dma((3,))],
        compiler_params=pltpu.CompilerParams(vmem_limit_bytes=24 * 2**20),
        name="finish",
    )(*new)
    return at_new.T, b_new, attended


def solution(mesh):
    return jax.shard_map(
        local,
        mesh=mesh,
        in_specs=(
            P("group", "blk"),
            P("group", "tensor"),
            P("blk", None),
            P(None, "tensor"),
            P("blk", "tensor"),
            P("group", "blk"),
            P(("group", "blk"), None, "tensor"),
            P(("group", "blk"), None, "tensor"),
            P(("group", "blk"), "tensor"),
            P(("group", "blk"), "tensor"),
            P(("group", "blk")),
        ),
        out_specs=(P("blk", None), P(None, "tensor"), P(("group", "blk"), "tensor")),
        check_vma=False,
    )
```

```python
import math

import jax
import jax.numpy as jnp
from jax import lax
from jax.experimental import pallas as pl
from jax.experimental.pallas import tpu as pltpu
from jax.sharding import PartitionSpec as P

MESH = pl.DeviceIdType.MESH
f32, bf16 = jnp.float32, jnp.bfloat16

adapter_scale = 2.0
learning_rate = 0.1
TOKENS = 2048
STEP = learning_rate * adapter_scale / TOKENS
OWNERS = 5
SHIFT = 2
FAR_FIRST = (4, 5, 3, 7, 6, 2, 1)
STAGES = ("p", "b1", "hx", "hx2", "a1", "a2", "a3", "b2", "hw", "a40", "a42", "a44", "a46", "u", "b3", "a5")


def split(v):
    hi = v.astype(bf16)
    return hi, (v - hi.astype(f32)).astype(bf16)


def dot_nt(p, q):
    return lax.dot_general(p, q, (((1,), (1,)), ((), ())), preferred_element_type=f32)


def dot_nn(p, q):
    return jnp.dot(p, q, preferred_element_type=f32)


def twice(dot, v, q):
    rows = v.shape[0]
    hi, lo = split(v)
    both = dot(jnp.concatenate([hi, lo], axis=0), q)
    return both[:rows] + both[rows:]


def exchange(
    x_any, c_any, at_any, b_any, w_any, h_any, k_any, v_any, ik_any, iv_any, len_any,
    at_out, b_out, att_out,
    x, c, at, bu, w, hid, kc, vc, ik, iv, lens,
    p_part, p_recv, a_part, a1_recv, a_half, a2_send, a2_recv,
    b_part, b1_recv, b_line, b_full,
    hw_part, hw_recv, hx_send, hx_recv, u_send, u_all, fold,
    in_sem, sems,
):
    g, t, b = lax.axis_index("group"), lax.axis_index("tensor"), lax.axis_index("blk")
    zh, y = lax.div(g, 8), lax.rem(g, 8)
    core = lax.rem(t, 2)
    z = zh * 4 + b
    y_first = core == 0
    m, n = jnp.where(y_first, y, z), jnp.where(y_first, z, y)

    def at_yt(dy, dt):
        return (zh * 8 + (y ^ dy), t ^ dt, b)

    def at_zt(dz, dt):
        far = z ^ dz
        return (lax.div(far, 4) * 8 + y, t ^ dt, lax.rem(far, 4))

    def at_y(d):
        return at_yt(d, 0)

    def at_z(d):
        return at_zt(d, 0)

    def at_t(d):
        return (g, t ^ d, b)

    def first(d):
        return tuple(jnp.where(y_first, p, q) for p, q in zip(at_y(d), at_z(d)))

    def second(d):
        return tuple(jnp.where(y_first, q, p) for p, q in zip(at_y(d), at_z(d)))

    barrier = pltpu.get_barrier_semaphore()
    for d in FAR_FIRST:
        for device in (at_t(d), at_y(d), at_z(d)):
            pl.semaphore_signal(barrier, inc=1, device_id=device, device_id_type=MESH)

    loads = [
        pltpu.make_async_copy(src, dst, in_sem.at[i])
        for i, (src, dst) in enumerate(
            zip(
                (c_any, b_any, x_any, at_any, h_any, w_any, k_any, v_any, ik_any, iv_any, len_any),
                (c, bu, x, at, hid, w, kc, vc, ik, iv, lens),
            )
        )
    ]
    for copy in loads:
        copy.start()

    def leaves(stage):
        return sems.at[2 * STAGES.index(stage)]

    def comes(stage):
        return sems.at[2 * STAGES.index(stage) + 1]

    def send(stage, src, dst, device):
        pltpu.make_async_remote_copy(
            src_ref=src, dst_ref=dst, send_sem=leaves(stage), recv_sem=comes(stage),
            device_id=device, device_id_type=MESH,
        ).start()

    def wait(sem, ref):
        pltpu.make_async_copy(ref, ref, sem).wait()

    def wait_if(case, sem, ref, otherwise):
        pl.when(case)(lambda: wait(sem, ref))
        if otherwise is not None:
            pl.when(jnp.logical_not(case))(lambda: wait(sem, otherwise))

    def rows(d):
        return pl.ds(pl.multiple_of(d * 8, 8), 8)

    def new_a(ranks, i):
        return at_out.at[rows(ranks), pl.ds(pl.multiple_of(i * 256, 256), 256)]

    def hidden_chunk(i):
        cols = pl.ds(i * 256, 256)
        hw_part[:, :, cols] = dot_nn(hid[...], w[:, cols]).reshape(4, 8, 256)

    loads[0].wait()
    loads[1].wait()
    p_part[...] = twice(dot_nt, bu[...], c[...]).reshape(8, 8, 128)

    loads[2].wait()
    loads[3].wait()
    low = twice(dot_nt, at[...], x[...])
    grad_b = twice(dot_nn, low, c[...])
    for i in range(8):
        for j in range(8):
            place = jnp.where(y_first, j * 8 + i, i * 8 + j)
            b_part[pl.ds(place, 1)] = grad_b[i * 8 : i * 8 + 8, j * 128 : j * 128 + 128].reshape(1, 8, 128)
    loads[4].wait()
    hx_send[...] = hid[...].astype(f32).reshape(8, 4, 1280)

    pl.semaphore_wait(barrier, 21)
    for d in FAR_FIRST:
        send("p", p_part.at[t ^ d], p_recv.at[d - 1], at_t(d))
    for d in FAR_FIRST:
        send("b1", b_part.at[rows(m ^ d)], b1_recv.at[d - 1], first(d))

    send("hx", hx_send.at[t], hx_recv.at[t], at_z(4))

    into = lax.broadcasted_iota(jnp.int32, (1024, 64), 0)
    out = lax.broadcasted_iota(jnp.int32, (1024, 64), 1)
    hit = (lax.div(into, 128) == lax.div(out, 8)) & (lax.rem(into, 8) == lax.rem(out, 8))
    fold[...] = jnp.where(hit, 1.0, 0.0).astype(bf16)

    loads[5].wait()
    hidden_chunk(0)
    hidden_chunk(1)

    wait(comes("p"), p_recv)
    back = p_part[t]
    for d in range(7):
        back = back + p_recv[d]
    grad_a = twice(dot_nn, back, x[...])
    for i in range(OWNERS):
        a_part[i] = grad_a[:, i * 256 : i * 256 + 256]

    def piece_of(place):
        return lax.rem(place + SHIFT, 8)

    owner = piece_of(y) < OWNERS
    piece = jnp.minimum(piece_of(y), OWNERS - 1)
    for d in FAR_FIRST:
        far = jnp.minimum(piece_of(y ^ d), OWNERS - 1)
        pl.when(piece_of(y ^ d) < OWNERS)(lambda d=d, far=far: send("a1", a_part.at[far], a1_recv.at[d - 1], at_y(d)))
    hidden_chunk(2)
    hidden_chunk(3)

    old = at[rows(t), pl.ds(pl.multiple_of(piece * 256, 256), 256)]

    @pl.when(owner)
    def _():
        wait(comes("a1"), a1_recv)
        total = a_part[piece]
        for d in range(7):
            total = total + a1_recv[d]
        a2_send[...] = total
        a_half[piece] = jnp.where(zh == 0, old, 0.0) - STEP * total
        for d in FAR_FIRST:
            send("a3", a_half.at[piece], a_half.at[piece], at_y(d))
        send("a2", a2_send, a2_recv, at_z(4))

    wait(comes("hx"), hx_recv.at[t])
    for d in FAR_FIRST:
        send("hx2", hx_recv.at[t], hx_recv.at[t], at_t(d))

    wait(comes("b1"), b1_recv)
    total = b_part[rows(m)]
    for d in range(7):
        total = total + b1_recv[d]
    b_line[n] = total
    for d in FAR_FIRST:
        send("b2", b_line.at[n], b_line.at[n], second(d))
    for d in (3, 2, 1):
        send("hw", hw_part.at[b ^ d], hw_recv.at[d - 1], at_z(d))

    @pl.when(owner)
    def _():
        wait(comes("a2"), a2_recv)
        at_out[rows(t), pl.ds(pl.multiple_of(piece * 256, 256), 256)] = old - STEP * (a2_send[...] + a2_recv[...])
        for dt in (4, 2, 6, 0):
            for d in FAR_FIRST + (0,):
                if d or dt:
                    send("a4" + str(dt), new_a(t, piece), new_a(t, piece), at_yt(d, dt))

    wait(comes("hx2"), hx_recv.at[pl.ds(0, 7)])
    both = jnp.concatenate([hid[...], hx_recv[...].reshape(32, 1280).astype(bf16)], axis=0)
    wait_if(owner, comes("a3"), a_half.at[pl.ds(0, OWNERS - 1)], a_half)
    near = jnp.zeros((64, 128), f32)
    for i in range(OWNERS):
        hi, lo = split(jnp.concatenate([a_half[i]] * 8, axis=0))
        near = near + dot_nt(both[:, i * 256 : i * 256 + 256], jnp.concatenate([hi, lo], axis=0))
    lane = lax.broadcasted_iota(jnp.int32, (64, 128), 1)
    row = lax.broadcasted_iota(jnp.int32, (64, 128), 0)
    near = jnp.where(lax.rem(lax.div(lane, 8), 8) == lax.rem(row, 8), near, 0.0).reshape(2, 4, 8, 128)
    near = jnp.sum(near, axis=2, keepdims=True)
    u_send[pl.ds(zh * 4, 4)] = near[0]
    u_send[pl.ds(4 - zh * 4, 4)] = near[1]
    u_all[t * 8 + z] = u_send[z]
    for dz in (4, 5, 3, 7, 6, 2, 1, 0):
        for dt in (4, 5, 2, 3, 6, 7, 1, 0):
            if dz or dt:
                copy = pltpu.make_async_remote_copy(
                    src_ref=u_send.at[z ^ dz], dst_ref=u_all.at[t * 8 + z], send_sem=leaves("u"), recv_sem=comes("u"),
                    device_id=at_zt(dz, dt), device_id_type=MESH,
                )
                copy.start()

    wait(comes("b2"), b_line.at[pl.ds(0, 7)])
    total = b_line[0]
    for i in range(1, 8):
        total = total + b_line[i]
    for i in range(8):
        line, col = jnp.where(y_first, i, m), jnp.where(y_first, m, i)
        tile = bu[rows(line), pl.ds(pl.multiple_of(col * 128, 128), 128)]
        b_full[m, i] = tile - STEP * total[i]
    for d in FAR_FIRST:
        send("b3", b_full.at[m], b_full.at[m], first(d))

    for i, dt in enumerate((0, 6, 2, 4)):
        if dt:
            wait(comes("a4" + str(dt)), at_out.at[rows(t ^ dt)])
        else:
            wait_if(owner, comes("a40"), at_out.at[pl.ds(0, 8), pl.ds(0, 1024)], at_out.at[rows(t)])
        send("a5", at_out.at[rows(t ^ dt)], at_out.at[rows(t ^ dt)], at_t(1))

    wait(comes("hw"), hw_recv)
    base = hw_part[b]
    for d in range(3):
        base = base + hw_recv[d]

    for copy in loads[6:]:
        copy.wait()
    row = lax.broadcasted_iota(jnp.int32, (8, 128), 0)
    slot = lax.broadcasted_iota(jnp.int32, (8, 128), 1)
    live = jnp.concatenate(
        [jnp.where((row == i) & (slot < lens[i]), 1.0, 0.0) for i in range(8)], axis=1
    )[None]
    live = jnp.broadcast_to(live, (8, 8, 1024)) > 0.5

    most = u_all.at[pl.ds(0, 63)]
    wait(comes("u"), most)
    slices = jnp.sum(u_all[...].reshape(8, 8, 1, 128), axis=1)
    lane = lax.broadcasted_iota(jnp.int32, (8, 128), 1)
    row = lax.broadcasted_iota(jnp.int32, (8, 128), 0)
    wide = jnp.concatenate(
        [jnp.where(lax.rem(lax.div(lane, 8), 8) == row, jnp.broadcast_to(slices[i], (8, 128)), 0.0) for i in range(8)], axis=1
    )
    hidden_low = twice(dot_nn, wide, fold[...])

    wait(comes("b3"), b_full.at[pl.ds(0, 7)])
    for i in range(8):
        for j in range(8):
            first_at, second_at = jnp.where(y_first, j, i), jnp.where(y_first, i, j)
            b_out[i * 8 : i * 8 + 8, j * 128 : j * 128 + 128] = b_full[first_at, second_at]

    b_hi, b_lo = split(b_out[...])
    hi, lo = split(hidden_low)
    both = dot_nn(jnp.concatenate([hi, lo], axis=0), b_hi)
    query = base + adapter_scale * (both[:8] + both[8:] + dot_nn(hi, b_lo))

    heads = jnp.concatenate([query[:, i * 128 : i * 128 + 128] for i in range(8)], axis=0).astype(bf16)
    scale = 1.0 / math.sqrt(128)
    scores = (dot_nt(heads, kc[...]) * scale).reshape(8, 8, 1024)
    scores = jnp.where(live, scores, -1e30)
    own_k = ik[...].astype(f32)[None]
    own = jnp.sum(heads.astype(f32).reshape(8, 8, 128) * own_k, axis=-1, keepdims=True) * scale
    peak = jnp.maximum(jnp.max(scores, axis=-1, keepdims=True), own)
    expo = jnp.where(live, jnp.exp(scores - peak), 0.0)
    own_expo = jnp.exp(own - peak)
    total = jnp.sum(expo, axis=-1, keepdims=True) + own_expo
    weights = (expo / total).astype(bf16).reshape(64, 1024)
    own_weight = (own_expo / total).astype(bf16).astype(f32)
    mixed = dot_nn(weights, vc[...]).reshape(8, 8, 128) + own_weight * iv[...].astype(f32)[None]
    mixed = mixed.astype(bf16)
    for i in range(8):
        att_out[:, i * 128 : i * 128 + 128] = mixed[i]

    wait(comes("a5"), at_out.at[pl.ds(0, 32)])

    for stage, ref in (
        ("p", p_recv), ("b1", b1_recv), ("hx", hx_recv.at[t]), ("hx2", hx_recv.at[pl.ds(0, 7)]),
        ("b2", b_line.at[pl.ds(0, 7)]), ("hw", hw_recv), ("u", most), ("b3", b_full.at[pl.ds(0, 7)]),
        ("a5", at_out.at[pl.ds(0, 32)]),
    ):
        wait(leaves(stage), ref)
    wait_if(owner, leaves("a1"), a_part.at[pl.ds(0, OWNERS - 1)], a_part)

    @pl.when(owner)
    def _():
        wait(leaves("a3"), a1_recv)
        wait(leaves("a2"), a2_recv)
        wait(leaves("a40"), a1_recv)
        for dt in (2, 4, 6):
            wait(leaves("a4" + str(dt)), b_line.at[pl.ds(0, 2)])


def finish(at_in, b_in, att_in, at_out, b_out, att_out, sem):
    stores = [
        pltpu.make_async_copy(src, dst, sem.at[i])
        for i, (src, dst) in enumerate(((at_in, at_out), (b_in, b_out), (att_in, att_out)))
    ]
    for copy in stores:
        copy.start()
    for copy in stores:
        copy.wait()


def local(x, c, a, bu, w, hid, keys, values, ik, iv, lens):
    vm, dma = pltpu.VMEM, pltpu.SemaphoreType.DMA
    slots = keys.shape[0] * keys.shape[1]
    hbm = pl.BlockSpec(memory_space=pltpu.HBM)
    vmem = pl.BlockSpec(memory_space=pltpu.VMEM)

    outs = (
        jax.ShapeDtypeStruct((64, 1280), f32),
        jax.ShapeDtypeStruct((64, 1024), f32),
        jax.ShapeDtypeStruct((8, 1024), bf16),
    )
    arrays = (x, c, a.T, bu, w, hid, keys.reshape(slots, 128), values.reshape(slots, 128), ik, iv, lens)
    new = pl.pallas_call(
        exchange,
        out_shape=outs,
        in_specs=[hbm] * 11,
        out_specs=(vmem,) * 3,
        scratch_shapes=[
            vm((128, 1280), bf16), vm((128, 1024), bf16), vm((64, 1280), f32), vm((64, 1024), f32),
            vm((1280, 1024), bf16), vm((32, 1280), bf16), vm((slots, 128), bf16), vm((slots, 128), bf16),
            vm((8, 128), bf16), vm((8, 128), bf16), pltpu.SMEM((8,), jnp.int32),
            vm((8, 8, 128), f32), vm((7, 8, 128), f32),
            vm((OWNERS, 8, 256), f32), vm((7, 8, 256), f32),
            vm((OWNERS, 8, 256), f32), vm((8, 256), f32), vm((8, 256), f32),
            vm((64, 8, 128), f32), vm((7, 8, 8, 128), f32), vm((8, 8, 8, 128), f32), vm((8, 8, 8, 128), f32),
            vm((4, 8, 1024), f32), vm((3, 8, 1024), f32),
            vm((8, 4, 1280), f32), vm((8, 4, 1280), f32),
            vm((8, 1, 128), f32), vm((64, 1, 128), f32), vm((1024, 64), bf16),
            dma((11,)), dma((2 * len(STAGES),)),
        ],
        compiler_params=pltpu.CompilerParams(
            collective_id=0, has_side_effects=True, vmem_limit_bytes=24 * 2**20
        ),
        name="exchange",
    )(*(pltpu.with_memory_space_constraint(v, pltpu.HBM) for v in arrays))
    at_new, b_new, attended = pl.pallas_call(
        finish,
        out_shape=outs,
        in_specs=[vmem] * 3,
        out_specs=(hbm,) * 3,
        scratch_shapes=[dma((3,))],
        compiler_params=pltpu.CompilerParams(vmem_limit_bytes=24 * 2**20),
        name="finish",
    )(*new)
    return at_new.T, b_new, attended


def solution(mesh):
    return jax.shard_map(
        local,
        mesh=mesh,
        in_specs=(
            P("group", "blk"),
            P("group", "tensor"),
            P("blk", None),
            P(None, "tensor"),
            P("blk", "tensor"),
            P("group", "blk"),
            P(("group", "blk"), None, "tensor"),
            P(("group", "blk"), None, "tensor"),
            P(("group", "blk"), "tensor"),
            P(("group", "blk"), "tensor"),
            P(("group", "blk")),
        ),
        out_specs=(P("blk", None), P(None, "tensor"), P(("group", "blk"), "tensor")),
        check_vma=False,
    )
```

```python
import math

import jax
import jax.numpy as jnp
from jax import lax
from jax.experimental import pallas as pl
from jax.experimental.pallas import tpu as pltpu
from jax.sharding import PartitionSpec as P

MESH = pl.DeviceIdType.MESH
f32, bf16 = jnp.float32, jnp.bfloat16

adapter_scale = 2.0
learning_rate = 0.1
TOKENS = 2048
STEP = learning_rate * adapter_scale / TOKENS
OWNERS = 5
SHIFT = 2
FAR_FIRST = (4, 5, 3, 7, 6, 2, 1)
STAGES = ("p", "b1", "hx", "hx2", "a1", "a2", "a3", "b2", "hw", "a40", "a42", "a44", "a46", "u", "b3", "a5")


def split(v):
    hi = v.astype(bf16)
    return hi, (v - hi.astype(f32)).astype(bf16)


def dot_nt(p, q):
    return lax.dot_general(p, q, (((1,), (1,)), ((), ())), preferred_element_type=f32)


def dot_nn(p, q):
    return jnp.dot(p, q, preferred_element_type=f32)


def twice(dot, v, q):
    rows = v.shape[0]
    hi, lo = split(v)
    both = dot(jnp.concatenate([hi, lo], axis=0), q)
    return both[:rows] + both[rows:]


def exchange(
    x_any, c_any, at_any, b_any, w_any, h_any, k_any, v_any, ik_any, iv_any, len_any,
    at_out, b_out, att_out,
    x, c, at, bu, w, hid, kc, vc, ik, iv, lens,
    p_part, p_recv, a_part, a1_recv, a_half, a2_send, a2_recv,
    b_part, b1_recv, b_line, b_full,
    hw_part, hw_recv, hx_send, hx_recv, u_send, u_all, fold,
    in_sem, sems,
):
    g, t, b = lax.axis_index("group"), lax.axis_index("tensor"), lax.axis_index("blk")
    zh, y = lax.div(g, 8), lax.rem(g, 8)
    core = lax.rem(t, 2)
    z = zh * 4 + b
    y_first = core == 0
    m, n = jnp.where(y_first, y, z), jnp.where(y_first, z, y)

    def at_yt(dy, dt):
        return (zh * 8 + (y ^ dy), t ^ dt, b)

    def at_zt(dz, dt):
        far = z ^ dz
        return (lax.div(far, 4) * 8 + y, t ^ dt, lax.rem(far, 4))

    def at_y(d):
        return at_yt(d, 0)

    def at_z(d):
        return at_zt(d, 0)

    def at_t(d):
        return (g, t ^ d, b)

    def first(d):
        return tuple(jnp.where(y_first, p, q) for p, q in zip(at_y(d), at_z(d)))

    def second(d):
        return tuple(jnp.where(y_first, q, p) for p, q in zip(at_y(d), at_z(d)))

    barrier = pltpu.get_barrier_semaphore()
    for d in FAR_FIRST:
        for device in (at_t(d), at_y(d), at_z(d)):
            pl.semaphore_signal(barrier, inc=1, device_id=device, device_id_type=MESH)

    loads = [
        pltpu.make_async_copy(src, dst, in_sem.at[i])
        for i, (src, dst) in enumerate(
            zip(
                (c_any, b_any, x_any, at_any, h_any, w_any, k_any, v_any, ik_any, iv_any, len_any),
                (c, bu, x, at, hid, w, kc, vc, ik, iv, lens),
            )
        )
    ]
    for copy in loads:
        copy.start()

    def leaves(stage):
        return sems.at[2 * STAGES.index(stage)]

    def comes(stage):
        return sems.at[2 * STAGES.index(stage) + 1]

    def send(stage, src, dst, device):
        pltpu.make_async_remote_copy(
            src_ref=src, dst_ref=dst, send_sem=leaves(stage), recv_sem=comes(stage),
            device_id=device, device_id_type=MESH,
        ).start()

    def wait(sem, ref):
        pltpu.make_async_copy(ref, ref, sem).wait()

    def wait_if(case, sem, ref, otherwise):
        pl.when(case)(lambda: wait(sem, ref))
        if otherwise is not None:
            pl.when(jnp.logical_not(case))(lambda: wait(sem, otherwise))

    def rows(d):
        return pl.ds(pl.multiple_of(d * 8, 8), 8)

    def new_a(ranks, i):
        return at_out.at[rows(ranks), pl.ds(pl.multiple_of(i * 256, 256), 256)]

    def hidden_chunk(i):
        cols = pl.ds(i * 256, 256)
        hw_part[:, :, cols] = dot_nn(hid[...], w[:, cols]).reshape(4, 8, 256)

    loads[0].wait()
    loads[1].wait()
    p_part[...] = twice(dot_nt, bu[...], c[...]).reshape(8, 8, 128)

    loads[2].wait()
    loads[3].wait()
    low = twice(dot_nt, at[...], x[...])
    grad_b = twice(dot_nn, low, c[...])
    for i in range(8):
        for j in range(8):
            place = jnp.where(y_first, j * 8 + i, i * 8 + j)
            b_part[pl.ds(place, 1)] = grad_b[i * 8 : i * 8 + 8, j * 128 : j * 128 + 128].reshape(1, 8, 128)
    loads[4].wait()
    hx_send[...] = hid[...].astype(f32).reshape(8, 4, 1280)

    pl.semaphore_wait(barrier, 21)
    for d in FAR_FIRST:
        send("p", p_part.at[t ^ d], p_recv.at[d - 1], at_t(d))
    for d in FAR_FIRST:
        send("b1", b_part.at[rows(m ^ d)], b1_recv.at[d - 1], first(d))

    send("hx", hx_send.at[t], hx_recv.at[t], at_z(4))

    into = lax.broadcasted_iota(jnp.int32, (1024, 64), 0)
    out = lax.broadcasted_iota(jnp.int32, (1024, 64), 1)
    hit = (lax.div(into, 128) == lax.div(out, 8)) & (lax.rem(into, 8) == lax.rem(out, 8))
    fold[...] = jnp.where(hit, 1.0, 0.0).astype(bf16)

    loads[5].wait()
    for i in range(4):
        hidden_chunk(i)

    wait(comes("p"), p_recv)
    back = p_part[t]
    for d in range(7):
        back = back + p_recv[d]
    grad_a = twice(dot_nn, back, x[...])
    for i in range(OWNERS):
        a_part[i] = grad_a[:, i * 256 : i * 256 + 256]

    def piece_of(place):
        return lax.rem(place + SHIFT, 8)

    owner = piece_of(y) < OWNERS
    piece = jnp.minimum(piece_of(y), OWNERS - 1)
    for d in FAR_FIRST:
        far = jnp.minimum(piece_of(y ^ d), OWNERS - 1)
        pl.when(piece_of(y ^ d) < OWNERS)(lambda d=d, far=far: send("a1", a_part.at[far], a1_recv.at[d - 1], at_y(d)))

    old = at[rows(t), pl.ds(pl.multiple_of(piece * 256, 256), 256)]

    @pl.when(owner)
    def _():
        wait(comes("a1"), a1_recv)
        total = a_part[piece]
        for d in range(7):
            total = total + a1_recv[d]
        a2_send[...] = total
        a_half[piece] = jnp.where(zh == 0, old, 0.0) - STEP * total
        for d in FAR_FIRST:
            send("a3", a_half.at[piece], a_half.at[piece], at_y(d))
        send("a2", a2_send, a2_recv, at_z(4))

    wait(comes("hx"), hx_recv.at[t])
    for d in FAR_FIRST:
        send("hx2", hx_recv.at[t], hx_recv.at[t], at_t(d))

    wait(comes("b1"), b1_recv)
    total = b_part[rows(m)]
    for d in range(7):
        total = total + b1_recv[d]
    b_line[n] = total
    for d in FAR_FIRST:
        send("b2", b_line.at[n], b_line.at[n], second(d))
    for d in (3, 2, 1):
        send("hw", hw_part.at[b ^ d], hw_recv.at[d - 1], at_z(d))

    @pl.when(owner)
    def _():
        wait(comes("a2"), a2_recv)
        at_out[rows(t), pl.ds(pl.multiple_of(piece * 256, 256), 256)] = old - STEP * (a2_send[...] + a2_recv[...])
        for dt in (0, 4, 2, 6):
            for d in FAR_FIRST + (0,):
                if d or dt:
                    send("a4" + str(dt), new_a(t, piece), new_a(t, piece), at_yt(d, dt))

    wait(comes("hx2"), hx_recv.at[pl.ds(0, 7)])
    both = jnp.concatenate([hid[...], hx_recv[...].reshape(32, 1280).astype(bf16)], axis=0)
    wait_if(owner, comes("a3"), a_half.at[pl.ds(0, OWNERS - 1)], a_half)
    near = jnp.zeros((64, 128), f32)
    for i in range(OWNERS):
        hi, lo = split(jnp.concatenate([a_half[i]] * 8, axis=0))
        near = near + dot_nt(both[:, i * 256 : i * 256 + 256], jnp.concatenate([hi, lo], axis=0))
    lane = lax.broadcasted_iota(jnp.int32, (64, 128), 1)
    row = lax.broadcasted_iota(jnp.int32, (64, 128), 0)
    near = jnp.where(lax.rem(lax.div(lane, 8), 8) == lax.rem(row, 8), near, 0.0).reshape(2, 4, 8, 128)
    near = jnp.sum(near, axis=2, keepdims=True)
    u_send[pl.ds(zh * 4, 4)] = near[0]
    u_send[pl.ds(4 - zh * 4, 4)] = near[1]
    u_all[t * 8 + z] = u_send[z]
    for dt in (4, 5, 2, 3, 6, 7, 1, 0):
        for dz in (4, 5, 3, 7, 6, 2, 1, 0):
            if dz or dt:
                copy = pltpu.make_async_remote_copy(
                    src_ref=u_send.at[z ^ dz], dst_ref=u_all.at[t * 8 + z], send_sem=leaves("u"), recv_sem=comes("u"),
                    device_id=at_zt(dz, dt), device_id_type=MESH,
                )
                copy.start()

    wait(comes("b2"), b_line.at[pl.ds(0, 7)])
    total = b_line[0]
    for i in range(1, 8):
        total = total + b_line[i]
    for i in range(8):
        line, col = jnp.where(y_first, i, m), jnp.where(y_first, m, i)
        tile = bu[rows(line), pl.ds(pl.multiple_of(col * 128, 128), 128)]
        b_full[m, i] = tile - STEP * total[i]
    for d in FAR_FIRST:
        send("b3", b_full.at[m], b_full.at[m], first(d))

    for i, dt in enumerate((0, 6, 2, 4)):
        if dt:
            wait(comes("a4" + str(dt)), at_out.at[rows(t ^ dt)])
        else:
            wait_if(owner, comes("a40"), at_out.at[pl.ds(0, 8), pl.ds(0, 1024)], at_out.at[rows(t)])
        send("a5", at_out.at[rows(t ^ dt)], at_out.at[rows(t ^ dt)], at_t(1))

    wait(comes("hw"), hw_recv)
    base = hw_part[b]
    for d in range(3):
        base = base + hw_recv[d]

    for copy in loads[6:]:
        copy.wait()
    row = lax.broadcasted_iota(jnp.int32, (8, 128), 0)
    slot = lax.broadcasted_iota(jnp.int32, (8, 128), 1)
    live = jnp.concatenate(
        [jnp.where((row == i) & (slot < lens[i]), 1.0, 0.0) for i in range(8)], axis=1
    )[None]
    live = jnp.broadcast_to(live, (8, 8, 1024)) > 0.5

    most = u_all.at[pl.ds(0, 63)]
    wait(comes("u"), most)
    slices = jnp.sum(u_all[...].reshape(8, 8, 1, 128), axis=1)
    lane = lax.broadcasted_iota(jnp.int32, (8, 128), 1)
    row = lax.broadcasted_iota(jnp.int32, (8, 128), 0)
    wide = jnp.concatenate(
        [jnp.where(lax.rem(lax.div(lane, 8), 8) == row, jnp.broadcast_to(slices[i], (8, 128)), 0.0) for i in range(8)], axis=1
    )
    hidden_low = twice(dot_nn, wide, fold[...])

    wait(comes("b3"), b_full.at[pl.ds(0, 7)])
    for i in range(8):
        for j in range(8):
            first_at, second_at = jnp.where(y_first, j, i), jnp.where(y_first, i, j)
            b_out[i * 8 : i * 8 + 8, j * 128 : j * 128 + 128] = b_full[first_at, second_at]

    b_hi, b_lo = split(b_out[...])
    hi, lo = split(hidden_low)
    both = dot_nn(jnp.concatenate([hi, lo], axis=0), b_hi)
    query = base + adapter_scale * (both[:8] + both[8:] + dot_nn(hi, b_lo))

    heads = jnp.concatenate([query[:, i * 128 : i * 128 + 128] for i in range(8)], axis=0).astype(bf16)
    scale = 1.0 / math.sqrt(128)
    scores = (dot_nt(heads, kc[...]) * scale).reshape(8, 8, 1024)
    scores = jnp.where(live, scores, -1e30)
    own_k = ik[...].astype(f32)[None]
    own = jnp.sum(heads.astype(f32).reshape(8, 8, 128) * own_k, axis=-1, keepdims=True) * scale
    peak = jnp.maximum(jnp.max(scores, axis=-1, keepdims=True), own)
    expo = jnp.where(live, jnp.exp(scores - peak), 0.0)
    own_expo = jnp.exp(own - peak)
    total = jnp.sum(expo, axis=-1, keepdims=True) + own_expo
    weights = (expo / total).astype(bf16).reshape(64, 1024)
    own_weight = (own_expo / total).astype(bf16).astype(f32)
    mixed = dot_nn(weights, vc[...]).reshape(8, 8, 128) + own_weight * iv[...].astype(f32)[None]
    mixed = mixed.astype(bf16)
    for i in range(8):
        att_out[:, i * 128 : i * 128 + 128] = mixed[i]

    wait(comes("a5"), at_out.at[pl.ds(0, 32)])

    for stage, ref in (
        ("p", p_recv), ("b1", b1_recv), ("hx", hx_recv.at[t]), ("hx2", hx_recv.at[pl.ds(0, 7)]),
        ("b2", b_line.at[pl.ds(0, 7)]), ("hw", hw_recv), ("u", most), ("b3", b_full.at[pl.ds(0, 7)]),
        ("a5", at_out.at[pl.ds(0, 32)]),
    ):
        wait(leaves(stage), ref)
    wait_if(owner, leaves("a1"), a_part.at[pl.ds(0, OWNERS - 1)], a_part)

    @pl.when(owner)
    def _():
        wait(leaves("a3"), a1_recv)
        wait(leaves("a2"), a2_recv)
        wait(leaves("a40"), a1_recv)
        for dt in (2, 4, 6):
            wait(leaves("a4" + str(dt)), b_line.at[pl.ds(0, 2)])


def finish(at_in, b_in, att_in, at_out, b_out, att_out, sem):
    stores = [
        pltpu.make_async_copy(src, dst, sem.at[i])
        for i, (src, dst) in enumerate(((at_in, at_out), (b_in, b_out), (att_in, att_out)))
    ]
    for copy in stores:
        copy.start()
    for copy in stores:
        copy.wait()


def local(x, c, a, bu, w, hid, keys, values, ik, iv, lens):
    vm, dma = pltpu.VMEM, pltpu.SemaphoreType.DMA
    slots = keys.shape[0] * keys.shape[1]
    hbm = pl.BlockSpec(memory_space=pltpu.HBM)
    vmem = pl.BlockSpec(memory_space=pltpu.VMEM)

    outs = (
        jax.ShapeDtypeStruct((64, 1280), f32),
        jax.ShapeDtypeStruct((64, 1024), f32),
        jax.ShapeDtypeStruct((8, 1024), bf16),
    )
    arrays = (x, c, a.T, bu, w, hid, keys.reshape(slots, 128), values.reshape(slots, 128), ik, iv, lens)
    new = pl.pallas_call(
        exchange,
        out_shape=outs,
        in_specs=[hbm] * 11,
        out_specs=(vmem,) * 3,
        scratch_shapes=[
            vm((128, 1280), bf16), vm((128, 1024), bf16), vm((64, 1280), f32), vm((64, 1024), f32),
            vm((1280, 1024), bf16), vm((32, 1280), bf16), vm((slots, 128), bf16), vm((slots, 128), bf16),
            vm((8, 128), bf16), vm((8, 128), bf16), pltpu.SMEM((8,), jnp.int32),
            vm((8, 8, 128), f32), vm((7, 8, 128), f32),
            vm((OWNERS, 8, 256), f32), vm((7, 8, 256), f32),
            vm((OWNERS, 8, 256), f32), vm((8, 256), f32), vm((8, 256), f32),
            vm((64, 8, 128), f32), vm((7, 8, 8, 128), f32), vm((8, 8, 8, 128), f32), vm((8, 8, 8, 128), f32),
            vm((4, 8, 1024), f32), vm((3, 8, 1024), f32),
            vm((8, 4, 1280), f32), vm((8, 4, 1280), f32),
            vm((8, 1, 128), f32), vm((64, 1, 128), f32), vm((1024, 64), bf16),
            dma((11,)), dma((2 * len(STAGES),)),
        ],
        compiler_params=pltpu.CompilerParams(
            collective_id=0, has_side_effects=True, vmem_limit_bytes=24 * 2**20
        ),
        name="exchange",
    )(*(pltpu.with_memory_space_constraint(v, pltpu.HBM) for v in arrays))
    at_new, b_new, attended = pl.pallas_call(
        finish,
        out_shape=outs,
        in_specs=[vmem] * 3,
        out_specs=(hbm,) * 3,
        scratch_shapes=[dma((3,))],
        compiler_params=pltpu.CompilerParams(vmem_limit_bytes=24 * 2**20),
        name="finish",
    )(*new)
    return at_new.T, b_new, attended


def solution(mesh):
    return jax.shard_map(
        local,
        mesh=mesh,
        in_specs=(
            P("group", "blk"),
            P("group", "tensor"),
            P("blk", None),
            P(None, "tensor"),
            P("blk", "tensor"),
            P("group", "blk"),
            P(("group", "blk"), None, "tensor"),
            P(("group", "blk"), None, "tensor"),
            P(("group", "blk"), "tensor"),
            P(("group", "blk"), "tensor"),
            P(("group", "blk")),
        ),
        out_specs=(P("blk", None), P(None, "tensor"), P(("group", "blk"), "tensor")),
        check_vma=False,
    )
```
